32 devices in a mesh: rep: 2 (over x), walk: 16 (over z, y, core).
Axes of the slice: x: 2, y: 2, z: 4, core: 2. Of those that a mesh axis runs over, the one named last changes fastest.
Arguments:
- greens: bfloat16 [32, 64, 384], P(('rep', 'walk')), parts along dimension 0, may hold values from -6 to 6
- source: int32 [64], P(('rep', 'walk')), parts along dimension 0, may hold values from 0 to 15, as said below
- counts: int32 [32], P('rep'), parts along dimension 0, may hold values from 1 to 2, as said below
- cholesky: bfloat16 [512, 64, 384], P('walk'), may hold values from -0.0390625 to 0.0390625
Outputs:
- relocated: bfloat16 [64, 64, 384], P(('rep', 'walk')), parts along dimension 0
- exchange_energy: float32 [64], P(('rep', 'walk')), parts along dimension 0
- force_bias: float32 [64, 512], P(('rep', 'walk')), parts along dimension 0
The draws below stay inside these ranges and needn't reach their ends.
There are 2 independent parts, one for each index of `rep`. The reference program is written for one: setup_inputs(seed, part) draws one part's arguments, and reference() takes and returns one part's arrays. A program takes and returns all parts, laid end to end along the dimension named above; an argument that names none is the same for every part. Nothing has to cross between parts.
Inputs may be any that keep to these rules, and one draw needn't show every extreme that they name: `source`: slot s belongs to walk device s div 2. Its walker comes from that device or one of the two devices beside it along the closed loop of walk devices. Slots beyond a device's count also name some walker. Slots 0 to counts[d] - 1 of device d are live.
All inputs are finite; a program needn't handle non-finite values.
Results may differ from the reference program's by a relative error of at most 0.001.
Values may be sent and summed in bfloat16 or wider, within the bound.
No kernel may reach another device: no remote copies, remote signals or barrier semaphores. Data moves between devices by JAX's collectives and lax.ppermute only.
A program may use at most 64 MiB of HBM per device.

```python
import jax
import jax.numpy as jnp
from jax import lax

NOCC = 64
NORB = 384
WSLOT = 1
CAP = 2
NW = 16
NW2 = 32
NCHOL = 512
N_WALK = 16


def population(key):
    base_key = jax.random.fold_in(key, 11)
    k_count, k_full, k_offset, k_local = jax.random.split(base_key, 4)
    counts = jax.random.randint(k_count, (N_WALK,), WSLOT, 2 * WSLOT + 1)
    fullest = jax.random.randint(k_full, (), 0, N_WALK)
    counts = counts.at[fullest].set(2 * WSLOT)
    counts = counts.at[(fullest + 1) % N_WALK].set(WSLOT)
    owner = jnp.arange(NW2) // CAP
    offset = jax.random.randint(k_offset, (NW2,), -1, 2)
    offset = offset.at[0].set(-1)
    offset = offset.at[CAP].set(-1)
    src_dev = (owner + offset) % N_WALK
    local_idx = jax.random.randint(k_local, (NW2,), 0, WSLOT)
    local_idx = local_idx.at[0].set(WSLOT - 1)
    local_idx = local_idx.at[CAP].set(0)
    source = (src_dev * WSLOT + local_idx).astype(jnp.int32)
    return (counts.astype(jnp.int32), source)


def draw_source(key, part):
    return population(key)[1]


def draw_counts(key, part):
    return population(key)[0]


def steps_of(own_key, shape, cuts, low, top_value):
    gain, own = 1.0, jax.random.fold_in(own_key, 6)
    for dim, blocks in cuts:
        draws = jnp.exp(jax.random.uniform(jax.random.fold_in(own, dim), (blocks,), jnp.float32, low / len(cuts), top_value / len(cuts)))
        gain = gain * jnp.repeat(draws, shape[dim] // blocks).reshape([-1 if axis == dim else 1 for axis in range(len(shape))])
    return gain


def normal_values(own_key, extent, scale, limit, pieces=(), held_as=jnp.bfloat16):
    gain = steps_of(own_key, extent, pieces, -0.22, 0.18) if pieces else 1.0
    values = jax.random.normal(own_key, extent, jnp.float32) * scale * gain
    return jnp.minimum(jnp.maximum(values, -limit), limit).astype(held_as)


def setup_inputs(seed: int = 0, part: int = 0) -> dict:
    keys = jax.random.split(jax.random.key(seed), 5)
    own_keys = jax.random.split(jax.random.fold_in(keys[4], part), 5)
    return {
        "greens": normal_values(own_keys[0], (NW, NOCC, NORB), 1.0, 6.0, ((0, 16),)),
        "source": draw_source(jax.random.fold_in(jax.random.fold_in(keys[4], part), 71), part),
        "counts": draw_counts(jax.random.fold_in(jax.random.fold_in(keys[4], part), 71), part),
        "cholesky": normal_values(keys[3], (NCHOL, NOCC, NORB), (NOCC * NORB) ** -0.5, 0.0390625, ((0, 16),)),
    }


def reference(greens, source, counts, cholesky):
    slot_pos = jnp.arange(NW2) % CAP
    owner = jnp.arange(NW2) // CAP
    is_live = slot_pos < counts[owner]
    relocated = jnp.where(is_live[:, None, None], greens[source], jnp.zeros((), jnp.bfloat16)).astype(jnp.bfloat16)
    chol_flat = cholesky.reshape(NCHOL * NOCC, NORB)

    def walker_energy(walker):
        rotated = jnp.dot(chol_flat, walker.T, preferred_element_type=jnp.float32).reshape(NCHOL, NOCC, NOCC)
        return -(0.5 / NCHOL) * jnp.sum(rotated * jnp.swapaxes(rotated, 1, 2))

    exchange_energy = lax.map(walker_energy, relocated)
    force_bias = jnp.dot(relocated.reshape(NW2, NOCC * NORB), cholesky.reshape(NCHOL, NOCC * NORB).T, preferred_element_type=jnp.float32)
    return relocated, exchange_energy, force_bias
```

```python
import functools

import jax
import jax.numpy as jnp
from jax import lax
from jax.experimental import pallas as pl
from jax.experimental.pallas import tpu as pltpu
from jax.sharding import PartitionSpec as P

ROWS = (((1,), (1,)), ((), ()))
LANES = 128
SUB = 8


def rows_dot(a, b):
    return lax.dot_general(a, b, ROWS, preferred_element_type=jnp.float32)


def interleaved(first, second, start, count):
    return jnp.concatenate([r[start + i] for i in range(count) for r in (first, second)], axis=0)


def fold(x):
    return jnp.sum(x.reshape(x.shape[0] // SUB, SUB, x.shape[1]), axis=0)


def block_sums(ga, gb, ca, cb, sums, width):
    pairs, occ, orb = ga.shape
    half = ca.shape[0]
    tile = 2 * occ
    lane = lax.broadcasted_iota(jnp.int32, (occ, tile), 1)
    row = lax.broadcasted_iota(jnp.int32, (occ, tile), 0)
    low = lane < occ
    eye = (lane == row) | (lane - occ == row)
    sums[2 * half :, :] = jnp.zeros((SUB, pairs * tile), jnp.float32)
    step_w = min(pairs, width)

    def chunk(k, _):
        start = pl.multiple_of(k * SUB, SUB)
        for w in range(0, pairs, step_w):
            traces = [[[] for _ in range(step_w)] for _ in range(2)]
            energy = [jnp.zeros((SUB, tile), jnp.float32) for _ in range(step_w)]
            for part in range(0, SUB, 4):
                at = start + part
                ce = ca[pl.ds(at, 4)].reshape(4 * occ, orb)
                co = cb[pl.ds(at, 4)].reshape(4 * occ, orb)
                ge = ga[w : w + step_w].reshape(step_w * occ, orb)
                go = gb[w : w + step_w].reshape(step_w * occ, orb)
                fe = rows_dot(ce, interleaved(ga, gb, w, step_w))
                fo = rows_dot(co, interleaved(gb, ga, w, step_w))
                me = rows_dot(ge, interleaved(ca, cb, at, 4))
                mo = rows_dot(go, interleaved(cb, ca, at, 4))
                for j in range(step_w):
                    cols = slice(j * tile, (j + 1) * tile)
                    rows_w = slice(j * occ, (j + 1) * occ)
                    odd = jnp.zeros((SUB, tile), jnp.float32)
                    for i in range(4):
                        rows_g = slice(i * occ, (i + 1) * occ)
                        cols_g = slice(i * tile, (i + 1) * tile)
                        f0, f1 = fe[rows_g, cols], fo[rows_g, cols]
                        m0, m1 = me[rows_w, cols_g], mo[rows_w, cols_g]
                        energy[j] += fold(f0 * jnp.where(low, m0, m1))
                        odd += fold(f1 * jnp.where(low, m1, m0))
                        traces[0][j].append(jnp.sum(fold(jnp.where(eye, f0, 0.0)), axis=0, keepdims=True))
                        traces[1][j].append(jnp.sum(fold(jnp.where(eye, f1, 0.0)), axis=0, keepdims=True))
                    energy[j] += pltpu.roll(odd, occ, 1)
            for j in range(step_w):
                cols = slice((w + j) * tile, (w + j + 1) * tile)
                sums[pl.ds(start, SUB), cols] = jnp.concatenate(traces[0][j], axis=0)
                odd = jnp.concatenate(traces[1][j], axis=0)
                sums[pl.ds(half + start, SUB), cols] = pltpu.roll(odd, occ, 1)
                sums[2 * half :, cols] += energy[j]
        return 0

    lax.fori_loop(0, half // SUB, chunk, 0)


def walker_rows(sums, occ):
    columns, lanes = sums.shape
    walkers = lanes // occ
    block = lax.broadcasted_iota(jnp.int32, (walkers, lanes), 1) // occ
    owner = lax.broadcasted_iota(jnp.int32, (walkers, lanes), 0)
    ones = (block == owner).astype(jnp.bfloat16)
    total = jnp.zeros((walkers, columns), jnp.float32)
    rest = sums
    for _ in range(3):
        part = rest.astype(jnp.bfloat16)
        total += rows_dot(ones, part)
        rest = rest - part.astype(jnp.float32)
    return total


def work_kernel(source, counts, greens, chol, relocated, sent, sums):
    walkers, occ, orb = greens.shape
    me = lax.axis_index("walk")
    slots = relocated.shape[0]
    live = counts[me]
    for t in range(slots):
        relocated[t] = jnp.where(t < live, greens[source[t]], jnp.zeros((), jnp.bfloat16))
    half = walkers // 2
    hc = chol.shape[0] // 2
    block_sums(greens.at[:half], greens.at[half:], chol.at[:hc], chol.at[hc:], sums, 4)
    rows = walker_rows(sums[...], occ)
    for lane in range(walkers):
        w = (lane // 2) + (lane % 2) * half
        row = rows[lane : lane + 1]
        for near in range(3):
            sent[(w + 1 - near) % walkers, near : near + 1, 0 : row.shape[1]] = row


def final_kernel(scale, source, counts, got, energy, bias):
    devices = got.shape[0]
    me = lax.axis_index("walk")
    slots = bias.shape[0]
    per = bias.shape[1] // devices
    live = counts[me]
    for t in range(slots):
        near = lax.rem(source[t] - me + 1 + devices, devices)
        rows = jnp.where(near == 0, got[:, 0, :], jnp.where(near == 1, got[:, 1, :], got[:, 2, :]))
        rows = jnp.where(t < live, rows, 0.0)
        bias[t : t + 1, :] = jnp.concatenate([rows[d : d + 1, :per] for d in range(devices)], axis=1)
        total = jnp.sum(rows[:, per : per + SUB])
        energy[t : t + 1, :] = jnp.full((1, LANES), total * scale)


def body(greens, source, counts, cholesky):
    devices = lax.axis_size("walk")
    chol_dev, occ, orb = cholesky.shape
    slots = source.shape[0]
    nchol = chol_dev * devices
    vmem = pl.BlockSpec(memory_space=pltpu.VMEM)
    smem = pl.BlockSpec(memory_space=pltpu.SMEM)
    params = pltpu.CompilerParams(vmem_limit_bytes=48 * 2**20)
    everyone = lax.all_gather(greens, "walk", axis=0, tiled=True)
    walkers = everyone.shape[0]
    relocated, sent = pl.pallas_call(
        work_kernel,
        out_shape=(
            jax.ShapeDtypeStruct((slots, occ, orb), jnp.bfloat16),
            jax.ShapeDtypeStruct((devices, 3, LANES), jnp.float32),
        ),
        in_specs=[smem, smem, vmem, vmem],
        out_specs=[vmem, vmem],
        scratch_shapes=[pltpu.VMEM((chol_dev + SUB, walkers * occ), jnp.float32)],
        compiler_params=params,
    )(source, counts, everyone, cholesky)
    got = lax.all_to_all(sent, "walk", split_axis=0, concat_axis=0, tiled=True)
    energy, bias = pl.pallas_call(
        functools.partial(final_kernel, -(0.5 / nchol)),
        out_shape=(
            jax.ShapeDtypeStruct((slots, LANES), jnp.float32),
            jax.ShapeDtypeStruct((slots, nchol), jnp.float32),
        ),
        in_specs=[smem, smem, vmem],
        out_specs=[vmem, vmem],
        compiler_params=params,
    )(source, counts, got)
    return relocated, energy[:, 0], bias


def solution(mesh):
    return jax.shard_map(
        body,
        mesh=mesh,
        in_specs=(
            P(("rep", "walk"), None, None),
            P(("rep", "walk")),
            P("rep"),
            P("walk", None, None),
        ),
        out_specs=(P(("rep", "walk"), None, None), P(("rep", "walk")), P(("rep", "walk"), None)),
        check_vma=False,
    )
```

```python
import functools

import jax
import jax.numpy as jnp
from jax import lax
from jax.experimental import pallas as pl
from jax.experimental.pallas import tpu as pltpu
from jax.sharding import PartitionSpec as P

ROWS = (((1,), (1,)), ((), ()))
LANES = 128
SUB = 8
NEAR = 3
STEP = 8


def rows_dot(a, b):
    return lax.dot_general(a, b, ROWS, preferred_element_type=jnp.float32)


def fold(x):
    return jnp.sum(x.reshape(x.shape[0] // SUB, SUB, x.shape[1]), axis=0)


def block_sums(blocks, ca, cb, sums, side, core):
    _, occ, orb = blocks[0].shape
    half = ca.shape[0]
    tile = 2 * occ
    lane = lax.broadcasted_iota(jnp.int32, (occ, tile), 1)
    row = lax.broadcasted_iota(jnp.int32, (occ, tile), 0)
    low = lane < occ
    eye = (lane == row) | (lane - occ == row)
    count = len(blocks)
    walkers = [jnp.concatenate(blocks[j : j + 2], axis=0).reshape(-1, orb) for j in range(0, count, 2)]
    spare = pl.ds(pl.multiple_of((1 - side) * 2 * half, 2 * half), 2 * half)
    sums[spare, :] = jnp.zeros((2 * half, count * tile), jnp.float32)

    def chunk(k, energies):
        energies = list(energies)
        start = pl.multiple_of(k * STEP, STEP)
        va = ca[pl.ds(start, STEP)].reshape(STEP * occ, orb)
        vb = cb[pl.ds(start, STEP)].reshape(STEP * occ, orb)
        for j in range(count):
            if j % 2 == 0:
                fa = rows_dot(va, walkers[j // 2])
                fb = rows_dot(vb, walkers[j // 2])
            cols = slice((j % 2) * tile, (j % 2 + 1) * tile)
            traces = [[], []]
            for i in range(STEP):
                rows = slice(i * occ, (i + 1) * occ)
                f0, f1 = fa[rows, cols], fb[rows, cols]
                turned = jnp.transpose(jnp.concatenate([f0, f1], axis=0))
                t0, t1 = turned[:occ], turned[occ:]
                crossed = pltpu.roll(jnp.where(low, t1, t0), occ, 1)
                energies[j] += fold(f0 * jnp.where(low, t0, crossed) + f1 * jnp.where(low, crossed, t1))
                for part, f in enumerate((f0, f1)):
                    traces[part].append(jnp.sum(fold(jnp.where(eye, f, 0.0)), axis=0, keepdims=True))
            for part in range(2):
                at = (2 * side + jnp.where(core == 0, part, 1 - part)) * half + start
                at = pl.ds(pl.multiple_of(at, STEP), STEP)
                sums[at, j * tile : (j + 1) * tile] = jnp.concatenate(traces[part], axis=0)
        return tuple(energies)

    zero = jnp.zeros((SUB, tile), jnp.float32)
    steps = half // STEP
    energies = lax.fori_loop(0, steps, chunk, (zero,) * count, unroll=steps if count <= 4 else 1)
    spare = pl.ds(pl.multiple_of((1 - side) * 2 * half, SUB), SUB)
    for j in range(count):
        sums[spare, j * tile : (j + 1) * tile] = energies[j]


def walker_rows(sums, occ):
    rows, lanes = sums.shape
    walkers = lanes // occ
    block = lax.broadcasted_iota(jnp.int32, (walkers, lanes), 1) // occ
    owner = lax.broadcasted_iota(jnp.int32, (walkers, lanes), 0)
    ones = (block == owner).astype(jnp.bfloat16)
    parts = []
    for _ in range(3):
        parts.append(sums.astype(jnp.bfloat16))
        sums = sums - parts[-1].astype(jnp.float32)
    total = rows_dot(ones, jnp.concatenate(parts, axis=0))
    return total[:, :rows] + total[:, rows : 2 * rows] + total[:, 2 * rows :]


def own_kernel(greens, partner, own):
    own[0] = greens[0]
    own[1] = partner[0]


def early_kernel(own, cross, block, mine, other, sums):
    me = lax.axis_index("walk")
    chip, core = me // 2, me % 2
    values = [jnp.concatenate([own[0:1], cross[...]], axis=0)] + [b[...] for b in block]
    block_sums(values, mine, other, sums, chip % 2, core)


def late_kernel(odds, far, half, forwarded, ca, cb, early, sent, sums):
    devices = sent.shape[0]
    occ = far.shape[1]
    me = lax.axis_index("walk")
    chip, core = me // 2, me % 2
    values = [jnp.concatenate([half[...], forwarded[...]], axis=0), far[...]]
    block_sums(values, ca, cb, sums, chip % 2, core)
    rows = walker_rows(jnp.concatenate([early[...], sums[...]], axis=1), occ)
    sent[...] = jnp.zeros_like(sent)
    plain = core == chip % 2
    walkers = [me, 2 * (chip ^ 1) + 1 - core]
    for s in odds:
        if s == 5:
            walkers += [me ^ 8, me ^ 10]
        else:
            there = chip ^ jnp.where(plain, s, s - 1)
            lead = jnp.where(plain, core, 1 - core)
            walkers += [2 * there + lead, 2 * there + 1 - lead]
    for r, walker in enumerate(walkers):
        for near in range(NEAR):
            sent[lax.rem(walker + 1 - near + devices, devices), near : near + 1, :] = rows[r : r + 1]


def relocate_kernel(shifts, source, counts, own, cross, *refs):
    blocks, (relocated, pick) = refs[:-2], refs[-2:]
    me = lax.axis_index("walk")
    chip, core = me // 2, me % 2
    devices = counts.shape[0]
    chips = devices // 2
    shift = chip ^ lax.rem(chip + jnp.where(core == 0, chips - 1, 1), chips)
    outer = cross[0]
    for s, block in zip(shifts, blocks):
        outer = jnp.where(shift == s, block[1], outer)
    row = lax.broadcasted_iota(jnp.int32, pick.shape[1:], 0)
    for t in range(relocated.shape[0]):
        near = lax.rem(source[t] - me + 1 + devices, devices)
        value = jnp.where(near == 1, own[0], jnp.where(near == 2 * core, outer, own[1]))
        relocated[t] = jnp.where(t < counts[me], value, jnp.zeros((), jnp.bfloat16))
        pick[t] = jnp.where((row == near) & (t < counts[me]), 1.0, 0.0)


def final_kernel(scale, pick, got, energy, bias):
    devices = got.shape[0]
    low = lax.broadcasted_iota(jnp.int32, pick.shape[1:], 1) < LANES // 2
    parts = jnp.zeros(pick.shape[1:], jnp.float32)
    for q in range(devices // 4):
        even = got[4 * q] + got[4 * q + 1]
        odd = got[4 * q + 2] + got[4 * q + 3]
        tile = jnp.where(low, even, odd)
        parts += jnp.where(low, odd, even)
        for t in range(bias.shape[0]):
            bias[t : t + 1, q * LANES : (q + 1) * LANES] = jnp.sum(tile * pick[t], axis=0, keepdims=True)
    for t in range(bias.shape[0]):
        energy[t] = jnp.sum(parts * pick[t]) * scale


def body(greens, source, counts, cholesky):
    devices = lax.axis_size("walk")
    chips = devices // 2
    chol_dev, occ, orb = cholesky.shape
    slots = source.shape[0]
    nchol = chol_dev * devices
    assert greens.shape[0] == 1 and 4 * chol_dev == LANES and 2 * occ == LANES
    assert chips >= 8 and chips & (chips - 1) == 0
    vmem = pl.BlockSpec(memory_space=pltpu.VMEM)
    smem = pl.BlockSpec(memory_space=pltpu.SMEM)
    params = pltpu.CompilerParams(vmem_limit_bytes=20 * 2**20)

    def permuted(x, source_of):
        return lax.ppermute(x, "walk", [(2 * n + k, 2 * m + c) for m in range(chips) for c in range(2) for n, k in [source_of(m, c)]])

    def trade(s):
        return permuted(own, lambda m, c: (m ^ s, c) if c == m % 2 else (m ^ (s - 1), 1 - c))

    partner = permuted(greens, lambda m, c: (m, 1 - c))
    half = permuted(greens, lambda m, c: (m ^ 4, c))
    cross = permuted(greens, lambda m, c: (m ^ 1, 1 - c))
    own = pl.pallas_call(
        own_kernel,
        out_shape=jax.ShapeDtypeStruct((2, occ, orb), greens.dtype),
        in_specs=[vmem, vmem],
        out_specs=vmem,
        compiler_params=params,
        cost_estimate=pl.CostEstimate(flops=4 * 10**9, bytes_accessed=4 * occ * orb, transcendentals=0),
    )(greens, partner)
    after_own, own = lax.optimization_barrier((cholesky, own))
    other = permuted(after_own, lambda m, c: (m, 1 - c))
    far = trade(7)
    beside = [trade(s) for s in [3] + list(range(9, chips, 2))]
    forwarded = permuted(half, lambda m, c: (m ^ 1, c))
    held = dict(zip([3] + list(range(9, chips, 2)) + [7], beside + [far]))
    odds = [3] + list(range(9, chips, 2)) + [5, 7]
    shifts = [2**k - 1 for k in range(2, chips.bit_length())]
    count = 1 + len(beside)

    def cost(blocks):
        flops = 2 * (2 * blocks * occ) * (2 * chol_dev * occ) * orb
        return pl.CostEstimate(flops=flops, bytes_accessed=4 * chol_dev * occ * orb, transcendentals=0)

    early = pl.pallas_call(
        lambda own, cross, *r: early_kernel(own, cross, r[: count - 1], *r[count - 1 :]),
        out_shape=jax.ShapeDtypeStruct((LANES, 2 * count * occ), jnp.float32),
        in_specs=[vmem] * (count + 3),
        out_specs=vmem,
        compiler_params=params,
        cost_estimate=cost(count),
    )(own, cross, *beside, cholesky, other)
    sent = pl.pallas_call(
        functools.partial(late_kernel, odds),
        out_shape=jax.ShapeDtypeStruct((devices, NEAR, LANES), jnp.float32),
        in_specs=[vmem] * 6,
        out_specs=vmem,
        scratch_shapes=[pltpu.VMEM((LANES, 4 * occ), jnp.float32)],
        compiler_params=params,
        cost_estimate=cost(2),
    )(far, half, forwarded, cholesky, other, early)
    got = lax.all_to_all(sent, "walk", split_axis=0, concat_axis=0, tiled=True)
    relocated, pick = pl.pallas_call(
        functools.partial(relocate_kernel, shifts),
        out_shape=(
            jax.ShapeDtypeStruct((slots, occ, orb), jnp.bfloat16),
            jax.ShapeDtypeStruct((slots, NEAR, LANES), jnp.float32),
        ),
        in_specs=[smem, smem] + [vmem] * (2 + len(shifts)),
        out_specs=[vmem, vmem],
        compiler_params=params,
    )(source, counts, own, cross, *[held[s] for s in shifts])
    energy, force_bias = pl.pallas_call(
        functools.partial(final_kernel, -(0.5 / nchol)),
        out_shape=(
            jax.ShapeDtypeStruct((slots,), jnp.float32),
            jax.ShapeDtypeStruct((slots, nchol), jnp.float32),
        ),
        in_specs=[vmem, vmem],
        out_specs=[smem, vmem],
        compiler_params=params,
    )(pick, got)
    return relocated, energy, force_bias


def solution(mesh):
    return jax.shard_map(
        body,
        mesh=mesh,
        in_specs=(
            P(("rep", "walk"), None, None),
            P(("rep", "walk")),
            P("rep"),
            P("walk", None, None),
        ),
        out_specs=(P(("rep", "walk"), None, None), P(("rep", "walk")), P(("rep", "walk"), None)),
        check_vma=False,
    )
```

```python
import functools

import jax
import jax.numpy as jnp
from jax import lax
from jax.experimental import pallas as pl
from jax.experimental.pallas import tpu as pltpu
from jax.sharding import PartitionSpec as P

ROWS = (((1,), (1,)), ((), ()))
LANES = 128
SUB = 8
NEAR = 3
STEP = 8


def rows_dot(a, b):
    return lax.dot_general(a, b, ROWS, preferred_element_type=jnp.float32)


def fold(x):
    return jnp.sum(x.reshape(x.shape[0] // SUB, SUB, x.shape[1]), axis=0)


def block_sums(blocks, ca, cb, sums, side, core):
    _, occ, orb = blocks[0].shape
    half = ca.shape[0]
    tile = 2 * occ
    lane = lax.broadcasted_iota(jnp.int32, (occ, tile), 1)
    row = lax.broadcasted_iota(jnp.int32, (occ, tile), 0)
    low = lane < occ
    eye = (lane == row) | (lane - occ == row)
    count = len(blocks)
    walkers = [jnp.concatenate(blocks[j : j + 2], axis=0).reshape(-1, orb) for j in range(0, count, 2)]
    spare = pl.ds(pl.multiple_of((1 - side) * 2 * half, 2 * half), 2 * half)
    sums[spare, :] = jnp.zeros((2 * half, count * tile), jnp.float32)

    def chunk(k, energies):
        energies = list(energies)
        start = pl.multiple_of(k * STEP, STEP)
        va = ca[pl.ds(start, STEP)].reshape(STEP * occ, orb)
        vb = cb[pl.ds(start, STEP)].reshape(STEP * occ, orb)
        for j in range(count):
            if j % 2 == 0:
                fa = rows_dot(va, walkers[j // 2])
                fb = rows_dot(vb, walkers[j // 2])
            cols = slice((j % 2) * tile, (j % 2 + 1) * tile)
            traces = [[], []]
            for i in range(STEP):
                rows = slice(i * occ, (i + 1) * occ)
                f0, f1 = fa[rows, cols], fb[rows, cols]
                turned = jnp.transpose(jnp.concatenate([f0, f1], axis=0))
                t0, t1 = turned[:occ], turned[occ:]
                crossed = pltpu.roll(jnp.where(low, t1, t0), occ, 1)
                energies[j] += fold(f0 * jnp.where(low, t0, crossed) + f1 * jnp.where(low, crossed, t1))
                for part, f in enumerate((f0, f1)):
                    traces[part].append(jnp.sum(fold(jnp.where(eye, f, 0.0)), axis=0, keepdims=True))
            for part in range(2):
                at = (2 * side + jnp.where(core == 0, part, 1 - part)) * half + start
                at = pl.ds(pl.multiple_of(at, STEP), STEP)
                sums[at, j * tile : (j + 1) * tile] = jnp.concatenate(traces[part], axis=0)
        return tuple(energies)

    zero = jnp.zeros((SUB, tile), jnp.float32)
    steps = half // STEP
    energies = lax.fori_loop(0, steps, chunk, (zero,) * count, unroll=steps if count <= 4 else 1)
    spare = pl.ds(pl.multiple_of((1 - side) * 2 * half, SUB), SUB)
    for j in range(count):
        sums[spare, j * tile : (j + 1) * tile] = energies[j]


def walker_rows(sums, occ):
    rows, lanes = sums.shape
    walkers = lanes // occ
    block = lax.broadcasted_iota(jnp.int32, (walkers, lanes), 1) // occ
    owner = lax.broadcasted_iota(jnp.int32, (walkers, lanes), 0)
    ones = (block == owner).astype(jnp.bfloat16)
    parts = []
    for _ in range(3):
        parts.append(sums.astype(jnp.bfloat16))
        sums = sums - parts[-1].astype(jnp.float32)
    total = rows_dot(ones, jnp.concatenate(parts, axis=0))
    return total[:, :rows] + total[:, rows : 2 * rows] + total[:, 2 * rows :]


def own_kernel(greens, partner, own):
    own[0] = greens[0]
    own[1] = partner[0]


def walker_ids(odds):
    me = lax.axis_index("walk")
    chip, core = me // 2, me % 2
    plain = core == chip % 2
    ids = []
    for s in odds:
        there = chip ^ jnp.where(plain, s, s - 1)
        lead = jnp.where(plain, core, 1 - core)
        ids += [2 * there + lead, 2 * there + 1 - lead]
    return ids


def send(sent, rows, ids):
    devices = sent.shape[0]
    for r, walker in enumerate(ids):
        for near in range(NEAR):
            sent[lax.rem(walker + 1 - near + devices, devices), near : near + 1, :] = rows[r : r + 1]


def early_kernel(odds, own, cross, *refs):
    blocks, (mine, other, blank, sent, sums) = refs[:-5], refs[-5:]
    me = lax.axis_index("walk")
    chip, core = me // 2, me % 2
    values = [jnp.concatenate([own[0:1], cross[...]], axis=0)] + [b[...] for b in blocks]
    block_sums(values, mine, other, sums, chip % 2, core)
    sent[...] = blank[...]
    rows = walker_rows(sums[...], own.shape[1])
    send(sent, rows, [me, 2 * (chip ^ 1) + 1 - core] + walker_ids(odds))


def next_kernel(block, mine, other, sums):
    me = lax.axis_index("walk")
    block_sums([block[...]], mine, other, sums, (me // 2) % 2, me % 2)


def late_kernel(odds, *refs):
    blocks, (mine, other, early, sent, sums) = refs[:-5], refs[-5:]
    me = lax.axis_index("walk")
    block_sums([b[...] for b in blocks], mine, other, sums, (me // 2) % 2, me % 2)
    sent[...] = early[...]
    send(sent, walker_rows(sums[...], blocks[0].shape[1]), walker_ids(odds))


def blank_kernel(sent):
    sent[...] = jnp.zeros_like(sent)


def pick_kernel(source, counts, pick):
    me = lax.axis_index("walk")
    devices = counts.shape[0]
    row = lax.broadcasted_iota(jnp.int32, pick.shape[1:], 0)
    for t in range(pick.shape[0]):
        near = lax.rem(source[t] - me + 1 + devices, devices)
        pick[t] = jnp.where((row == near) & (t < counts[me]), 1.0, 0.0)


def relocate(shifts, pick, own, cross, blocks, relocated):
    me = lax.axis_index("walk")
    chip, core = me // 2, me % 2
    chips = lax.axis_size("walk") // 2
    shift = chip ^ lax.rem(chip + jnp.where(core == 0, chips - 1, 1), chips)
    outer = cross[0]
    for s, block in zip(shifts, blocks):
        outer = jnp.where(shift == s, block[1], outer)
    before, after = jnp.where(core == 0, outer, own[1]), jnp.where(core == 0, own[1], outer)
    for t in range(relocated.shape[0]):
        value = jnp.zeros(relocated.shape[1:], jnp.float32)
        for near, walker in enumerate((before, own[0], after)):
            weight = jnp.concatenate([pick[t, near : near + 1]] * (relocated.shape[2] // LANES), axis=1)
            value = jnp.where(weight > 0, walker.astype(jnp.float32), value)
        relocated[t] = value.astype(relocated.dtype)


def relocate_kernel(shifts, pick, own, cross, *refs):
    relocate(shifts, pick, own, cross, refs[:-1], refs[-1])


def final_kernel(scale, shifts, pick, got, own, cross, *refs):
    blocks, (relocated, energy, bias) = refs[:-3], refs[-3:]
    relocate(shifts, pick, own, cross, blocks, relocated)
    devices = got.shape[0]
    low = lax.broadcasted_iota(jnp.int32, pick.shape[1:], 1) < LANES // 2
    parts = jnp.zeros(pick.shape[1:], jnp.float32)
    for q in range(devices // 4):
        even = got[4 * q] + got[4 * q + 1]
        odd = got[4 * q + 2] + got[4 * q + 3]
        tile = jnp.where(low, even, odd)
        parts += jnp.where(low, odd, even)
        for t in range(bias.shape[0]):
            bias[t : t + 1, q * LANES : (q + 1) * LANES] = jnp.sum(tile * pick[t], axis=0, keepdims=True)
    for t in range(bias.shape[0]):
        energy[t] = jnp.sum(parts * pick[t]) * scale


def body(greens, source, counts, cholesky):
    devices = lax.axis_size("walk")
    chips = devices // 2
    chol_dev, occ, orb = cholesky.shape
    slots = source.shape[0]
    nchol = chol_dev * devices
    assert greens.shape[0] == 1 and 4 * chol_dev == LANES and 2 * occ == LANES
    assert chips >= 8 and chips & (chips - 1) == 0
    vmem = pl.BlockSpec(memory_space=pltpu.VMEM)
    smem = pl.BlockSpec(memory_space=pltpu.SMEM)
    params = pltpu.CompilerParams(vmem_limit_bytes=20 * 2**20)

    def permuted(x, source_of):
        return lax.ppermute(x, "walk", [(2 * n + k, 2 * m + c) for m in range(chips) for c in range(2) for n, k in [source_of(m, c)]])

    def trade(s):
        return permuted(own, lambda m, c: (m ^ s, c) if c == m % 2 else (m ^ (s - 1), 1 - c))

    partner = permuted(greens, lambda m, c: (m, 1 - c))
    payload = jax.ShapeDtypeStruct((devices, NEAR, LANES), jnp.float32)
    blank = pl.pallas_call(
        blank_kernel,
        out_shape=payload,
        out_specs=vmem,
        compiler_params=params,
        cost_estimate=pl.CostEstimate(flops=4 * 10**9, bytes_accessed=4096, transcendentals=0),
    )()
    partner, blank = lax.optimization_barrier((partner, blank))
    own = pl.pallas_call(
        own_kernel,
        out_shape=jax.ShapeDtypeStruct((2, occ, orb), greens.dtype),
        in_specs=[vmem, vmem],
        out_specs=vmem,
        compiler_params=params,
        cost_estimate=pl.CostEstimate(flops=0, bytes_accessed=4 * occ * orb, transcendentals=0),
    )(greens, partner)
    after_own, own = lax.optimization_barrier((cholesky, own))
    other = permuted(after_own, lambda m, c: (m, 1 - c))
    odds = [7] + list(range(9, chips, 2))
    trades = [trade(s) for s in odds]
    near = trade(3)
    after, own = lax.optimization_barrier((greens, own))
    cross = permuted(after, lambda m, c: (m ^ 1, 1 - c))
    last = trade(5)
    held = dict(zip(odds + [3], trades + [near]))
    shifts = [2**k - 1 for k in range(2, chips.bit_length())]
    count = 1 + len(trades)

    def compute(kernel, out_shape, blocks, operands, scratch):
        flops = 2 * (2 * blocks * occ) * (2 * chol_dev * occ) * orb
        return pl.pallas_call(
            kernel,
            out_shape=out_shape,
            in_specs=[vmem] * len(operands),
            out_specs=vmem,
            scratch_shapes=[sums_of(blocks, pltpu.VMEM)] if scratch else [],
            compiler_params=params,
            cost_estimate=pl.CostEstimate(flops=flops, bytes_accessed=4 * chol_dev * occ * orb, transcendentals=0),
        )(*operands)

    def sums_of(blocks, kind):
        return kind((LANES, 2 * blocks * occ), jnp.float32)

    pick = pl.pallas_call(
        pick_kernel,
        out_shape=jax.ShapeDtypeStruct((slots, NEAR, LANES), jnp.float32),
        in_specs=[smem, smem],
        out_specs=vmem,
        compiler_params=params,
        cost_estimate=pl.CostEstimate(flops=4 * 10**9, bytes_accessed=4096, transcendentals=0),
    )(source, counts)
    held_own = own
    own, pick = lax.optimization_barrier((own, pick))
    early = compute(functools.partial(early_kernel, odds), payload, count, (own, cross, *trades, cholesky, other, blank), True)
    sent = compute(functools.partial(late_kernel, [3, 5]), payload, 2, (near, last, cholesky, other, early), True)
    got = lax.all_to_all(sent, "walk", split_axis=0, concat_axis=0, tiled=True)
    relocated, energy, force_bias = pl.pallas_call(
        functools.partial(final_kernel, -(0.5 / nchol), shifts),
        out_shape=(
            jax.ShapeDtypeStruct((slots, occ, orb), greens.dtype),
            jax.ShapeDtypeStruct((slots,), jnp.float32),
            jax.ShapeDtypeStruct((slots, nchol), jnp.float32),
        ),
        in_specs=[vmem] * (4 + len(shifts)),
        out_specs=[vmem, smem, vmem],
        compiler_params=params,
    )(pick, got, own, cross, *[held[s] for s in shifts])
    return relocated, energy, force_bias


def solution(mesh):
    return jax.shard_map(
        body,
        mesh=mesh,
        in_specs=(
            P(("rep", "walk"), None, None),
            P(("rep", "walk")),
            P("rep"),
            P("walk", None, None),
        ),
        out_specs=(P(("rep", "walk"), None, None), P(("rep", "walk")), P(("rep", "walk"), None)),
        check_vma=False,
    )
```

```python
import functools

import jax
import jax.numpy as jnp
from jax import lax
from jax.experimental import pallas as pl
from jax.experimental.pallas import tpu as pltpu
from jax.sharding import PartitionSpec as P

ROWS = (((1,), (1,)), ((), ()))
LANES = 128
SUB = 8
NEAR = 3
SINGLES = {"own": 0, "cross": 3, "half": 8, "forwarded": 10}
STEP = 8


def rows_dot(a, b):
    return lax.dot_general(a, b, ROWS, preferred_element_type=jnp.float32)


def fold(x):
    return jnp.sum(x.reshape(x.shape[0] // SUB, SUB, x.shape[1]), axis=0)


def block_sums(blocks, ca, cb, sums, side, core):
    _, occ, orb = blocks[0].shape
    half = ca.shape[0]
    tile = 2 * occ
    lane = lax.broadcasted_iota(jnp.int32, (occ, tile), 1)
    row = lax.broadcasted_iota(jnp.int32, (occ, tile), 0)
    low = lane < occ
    eye = (lane == row) | (lane - occ == row)
    count = len(blocks)
    walkers = [jnp.concatenate(blocks[j : j + 2], axis=0).reshape(-1, orb) for j in range(0, count, 2)]
    spare = pl.ds(pl.multiple_of((1 - side) * 2 * half, 2 * half), 2 * half)
    sums[spare, :] = jnp.zeros((2 * half, count * tile), jnp.float32)

    def chunk(k, energies):
        energies = list(energies)
        start = pl.multiple_of(k * STEP, STEP)
        va = ca[pl.ds(start, STEP)].reshape(STEP * occ, orb)
        vb = cb[pl.ds(start, STEP)].reshape(STEP * occ, orb)
        for j in range(count):
            if j % 2 == 0:
                fa = rows_dot(va, walkers[j // 2])
                fb = rows_dot(vb, walkers[j // 2])
            cols = slice((j % 2) * tile, (j % 2 + 1) * tile)
            traces = [[], []]
            for i in range(STEP):
                rows = slice(i * occ, (i + 1) * occ)
                f0, f1 = fa[rows, cols], fb[rows, cols]
                turned = jnp.transpose(jnp.concatenate([f0, f1], axis=0))
                t0, t1 = turned[:occ], turned[occ:]
                crossed = pltpu.roll(jnp.where(low, t1, t0), occ, 1)
                energies[j] += fold(f0 * jnp.where(low, t0, crossed) + f1 * jnp.where(low, crossed, t1))
                for part, f in enumerate((f0, f1)):
                    traces[part].append(jnp.sum(fold(jnp.where(eye, f, 0.0)), axis=0, keepdims=True))
            for part in range(2):
                at = (2 * side + jnp.where(core == 0, part, 1 - part)) * half + start
                at = pl.ds(pl.multiple_of(at, STEP), STEP)
                sums[at, j * tile : (j + 1) * tile] = jnp.concatenate(traces[part], axis=0)
        return tuple(energies)

    zero = jnp.zeros((SUB, tile), jnp.float32)
    steps = half // STEP
    energies = lax.fori_loop(0, steps, chunk, (zero,) * count, unroll=steps if count <= 4 else 1)
    spare = pl.ds(pl.multiple_of((1 - side) * 2 * half, SUB), SUB)
    for j in range(count):
        sums[spare, j * tile : (j + 1) * tile] = energies[j]


def walker_rows(sums, occ):
    rows, lanes = sums.shape
    walkers = lanes // occ
    block = lax.broadcasted_iota(jnp.int32, (walkers, lanes), 1) // occ
    owner = lax.broadcasted_iota(jnp.int32, (walkers, lanes), 0)
    ones = (block == owner).astype(jnp.bfloat16)
    parts = []
    for _ in range(3):
        parts.append(sums.astype(jnp.bfloat16))
        sums = sums - parts[-1].astype(jnp.float32)
    total = rows_dot(ones, jnp.concatenate(parts, axis=0))
    return total[:, :rows] + total[:, rows : 2 * rows] + total[:, 2 * rows :]


def own_kernel(greens, partner, own):
    own[0] = greens[0]
    own[1] = partner[0]


def walker_ids(tiles):
    me = lax.axis_index("walk")
    chip, core = me // 2, me % 2
    plain = core == chip % 2
    ids = []
    for tile in tiles:
        if isinstance(tile, tuple):
            ids += [me ^ SINGLES[name] for name in tile]
        else:
            there = chip ^ jnp.where(plain, tile, tile - 1)
            lead = jnp.where(plain, core, 1 - core)
            ids += [2 * there + lead, 2 * there + 1 - lead]
    return ids


def values_of(tiles, refs):
    refs = list(refs)
    values = []
    for tile in tiles:
        if isinstance(tile, tuple):
            values.append(jnp.stack([refs.pop(0)[0] for _ in tile]))
        else:
            values.append(refs.pop(0)[...])
    return values


def send(sent, rows, ids):
    devices = sent.shape[0]
    for r, walker in enumerate(ids):
        for near in range(NEAR):
            sent[lax.rem(walker + 1 - near + devices, devices), near : near + 1, :] = rows[r : r + 1]


def compute_kernel(tiles, *refs):
    blocks, (mine, other, before, sent, sums) = refs[:-5], refs[-5:]
    me = lax.axis_index("walk")
    block_sums(values_of(tiles, blocks), mine, other, sums, (me // 2) % 2, me % 2)
    sent[...] = before[...]
    send(sent, walker_rows(sums[...], blocks[0].shape[1]), walker_ids(tiles))


def copy_kernel(x, y):
    y[...] = x[...]


def blank_kernel(sent):
    sent[...] = jnp.zeros_like(sent)


def picks(source, counts, slots):
    me = lax.axis_index("walk")
    devices = counts.shape[1]
    count = jnp.sum(jnp.where(lax.broadcasted_iota(jnp.int32, counts.shape, 1) == me, counts[...], 0), axis=1, keepdims=True)
    row = lax.broadcasted_iota(jnp.int32, (NEAR, LANES), 0)
    found = []
    for t in range(slots):
        walker = jnp.where(lax.broadcasted_iota(jnp.int32, source.shape, 1) == t, source[...], 0)
        near = jnp.sum(walker, axis=1, keepdims=True) - me + 1
        near = jnp.where(near < 0, near + devices, jnp.where(near >= devices, near - devices, near))
        found.append(jnp.where((row == near) & (count > t), 1.0, 0.0))
    return found


def relocate(shifts, pick, own, cross, blocks, relocated):
    me = lax.axis_index("walk")
    chip, core = me // 2, me % 2
    chips = lax.axis_size("walk") // 2
    shift = chip ^ lax.rem(chip + jnp.where(core == 0, chips - 1, 1), chips)
    outer = cross[0]
    for s, block in zip(shifts, blocks):
        outer = jnp.where(shift == s, block[1], outer)
    before, after = jnp.where(core == 0, outer, own[1]), jnp.where(core == 0, own[1], outer)
    for t in range(relocated.shape[0]):
        value = jnp.zeros(relocated.shape[1:], jnp.float32)
        for near, walker in enumerate((before, own[0], after)):
            weight = jnp.concatenate([pick[t][near : near + 1]] * (relocated.shape[2] // LANES), axis=1)
            value = jnp.where(weight > 0, walker.astype(jnp.float32), value)
        relocated[t] = value.astype(relocated.dtype)


def relocate_kernel(shifts, pick, own, cross, *refs):
    relocate(shifts, pick, own, cross, refs[:-1], refs[-1])


def final_kernel(scale, shifts, source, counts, got, own, cross, *refs):
    pick = picks(source, counts, refs[-1].shape[0])
    blocks, (relocated, energy, bias) = refs[:-3], refs[-3:]
    relocate(shifts, pick, own, cross, blocks, relocated)
    devices = got.shape[0]
    low = lax.broadcasted_iota(jnp.int32, pick[0].shape, 1) < LANES // 2
    parts = jnp.zeros(pick[0].shape, jnp.float32)
    for q in range(devices // 4):
        even = got[4 * q] + got[4 * q + 1]
        odd = got[4 * q + 2] + got[4 * q + 3]
        tile = jnp.where(low, even, odd)
        parts += jnp.where(low, odd, even)
        for t in range(bias.shape[0]):
            bias[t : t + 1, q * LANES : (q + 1) * LANES] = jnp.sum(tile * pick[t], axis=0, keepdims=True)
    for t in range(bias.shape[0]):
        energy[t] = jnp.sum(parts * pick[t]) * scale


def body(greens, source, counts, cholesky):
    devices = lax.axis_size("walk")
    chips = devices // 2
    chol_dev, occ, orb = cholesky.shape
    slots = source.shape[0]
    nchol = chol_dev * devices
    assert greens.shape[0] == 1 and 4 * chol_dev == LANES and 2 * occ == LANES
    assert chips >= 8 and chips & (chips - 1) == 0
    vmem = pl.BlockSpec(memory_space=pltpu.VMEM)
    smem = pl.BlockSpec(memory_space=pltpu.SMEM)
    params = pltpu.CompilerParams(vmem_limit_bytes=20 * 2**20)

    def permuted(x, source_of):
        return lax.ppermute(x, "walk", [(2 * n + k, 2 * m + c) for m in range(chips) for c in range(2) for n, k in [source_of(m, c)]])

    def trade(s):
        return permuted(own, lambda m, c: (m ^ s, c) if c == m % 2 else (m ^ (s - 1), 1 - c))

    partner = permuted(greens, lambda m, c: (m, 1 - c))
    payload = jax.ShapeDtypeStruct((devices, NEAR, LANES), jnp.float32)
    half = permuted(greens, lambda m, c: (m ^ 4, c))
    blank = pl.pallas_call(
        blank_kernel,
        out_shape=payload,
        out_specs=vmem,
        compiler_params=params,
        cost_estimate=pl.CostEstimate(flops=4 * 10**9, bytes_accessed=4096, transcendentals=0),
    )()
    partner, blank = lax.optimization_barrier((partner, blank))
    own = pl.pallas_call(
        own_kernel,
        out_shape=jax.ShapeDtypeStruct((2, occ, orb), greens.dtype),
        in_specs=[vmem, vmem],
        out_specs=vmem,
        compiler_params=params,
        cost_estimate=pl.CostEstimate(flops=0, bytes_accessed=4 * occ * orb, transcendentals=0),
    )(greens, partner)
    after_own, own = lax.optimization_barrier((cholesky, own))
    other = permuted(after_own, lambda m, c: (m, 1 - c))
    far = trade(7)
    near = trade(3)
    more = list(range(9, chips, 2))
    held = {7: far, 3: near, **{s: trade(s) for s in more}}
    forwarded = permuted(half, lambda m, c: (m ^ 1, c))
    cross = permuted(greens, lambda m, c: (m ^ 1, 1 - c))
    shifts = [2**k - 1 for k in range(2, chips.bit_length())]
    blank = pl.pallas_call(
        copy_kernel,
        out_shape=payload,
        in_specs=[vmem],
        out_specs=vmem,
        compiler_params=params,
        cost_estimate=pl.CostEstimate(flops=4 * 10**9, bytes_accessed=4096, transcendentals=0),
    )(blank)
    singles = {"own": own, "cross": cross, "half": half, "forwarded": forwarded}

    def compute(tiles, before):
        flops = 2 * (2 * len(tiles) * occ) * (2 * chol_dev * occ) * orb
        operands = []
        for tile in tiles:
            operands += [singles[name] for name in tile] if isinstance(tile, tuple) else [held[tile]]
        operands += [cholesky, other, before]
        return pl.pallas_call(
            functools.partial(compute_kernel, tiles),
            out_shape=payload,
            in_specs=[vmem] * len(operands),
            out_specs=vmem,
            scratch_shapes=[pltpu.VMEM((LANES, 2 * len(tiles) * occ), jnp.float32)],
            compiler_params=params,
            cost_estimate=pl.CostEstimate(flops=flops, bytes_accessed=4 * chol_dev * occ * orb, transcendentals=0),
        )(*operands)

    sent = compute([("own","half"),3] + more, blank)
    sent = compute([7,("cross","forwarded")], sent)
    got = lax.all_to_all(sent, "walk", split_axis=0, concat_axis=0, tiled=True)
    relocated, energy, force_bias = pl.pallas_call(
        functools.partial(final_kernel, -(0.5 / nchol), shifts),
        out_shape=(
            jax.ShapeDtypeStruct((slots, occ, orb), greens.dtype),
            jax.ShapeDtypeStruct((slots,), jnp.float32),
            jax.ShapeDtypeStruct((slots, nchol), jnp.float32),
        ),
        in_specs=[vmem] * (5 + len(shifts)),
        out_specs=[vmem, smem, vmem],
        compiler_params=params,
    )(source.reshape(1, -1), counts.reshape(1, -1), got, own, cross, *[held[s] for s in shifts])
    return relocated, energy, force_bias


def solution(mesh):
    return jax.shard_map(
        body,
        mesh=mesh,
        in_specs=(
            P(("rep", "walk"), None, None),
            P(("rep", "walk")),
            P("rep"),
            P("walk", None, None),
        ),
        out_specs=(P(("rep", "walk"), None, None), P(("rep", "walk")), P(("rep", "walk"), None)),
        check_vma=False,
    )
```

```python
import functools

import jax
import jax.numpy as jnp
from jax import lax
from jax.experimental import pallas as pl
from jax.experimental.pallas import tpu as pltpu
from jax.sharding import PartitionSpec as P

ROWS = (((1,), (1,)), ((), ()))
LANES = 128
SUB = 8
NEAR = 3
SINGLES = {"own": 0, "cross": 3, "half": 8, "forwarded": 10}
STEP = 8


def rows_dot(a, b):
    return lax.dot_general(a, b, ROWS, preferred_element_type=jnp.float32)


def fold(x):
    return jnp.sum(x.reshape(x.shape[0] // SUB, SUB, x.shape[1]), axis=0)


def block_sums(blocks, ca, cb, sums, side, core):
    _, occ, orb = blocks[0].shape
    half = ca.shape[0]
    tile = 2 * occ
    lane = lax.broadcasted_iota(jnp.int32, (occ, tile), 1)
    row = lax.broadcasted_iota(jnp.int32, (occ, tile), 0)
    low = lane < occ
    eye = (lane == row) | (lane - occ == row)
    count = len(blocks)
    walkers = [jnp.concatenate(blocks[j : j + 2], axis=0).reshape(-1, orb) for j in range(0, count, 2)]
    spare = pl.ds(pl.multiple_of((1 - side) * 2 * half, 2 * half), 2 * half)
    sums[spare, :] = jnp.zeros((2 * half, count * tile), jnp.float32)

    def chunk(k, energies):
        energies = list(energies)
        start = pl.multiple_of(k * STEP, STEP)
        va = ca[pl.ds(start, STEP)].reshape(STEP * occ, orb)
        vb = cb[pl.ds(start, STEP)].reshape(STEP * occ, orb)
        for j in range(count):
            if j % 2 == 0:
                fa = rows_dot(va, walkers[j // 2])
                fb = rows_dot(vb, walkers[j // 2])
            cols = slice((j % 2) * tile, (j % 2 + 1) * tile)
            traces = [[], []]
            for i in range(STEP):
                rows = slice(i * occ, (i + 1) * occ)
                f0, f1 = fa[rows, cols], fb[rows, cols]
                turned = jnp.transpose(jnp.concatenate([f0, f1], axis=0))
                t0, t1 = turned[:occ], turned[occ:]
                crossed = pltpu.roll(jnp.where(low, t1, t0), occ, 1)
                energies[j] += fold(f0 * jnp.where(low, t0, crossed) + f1 * jnp.where(low, crossed, t1))
                for part, f in enumerate((f0, f1)):
                    traces[part].append(jnp.sum(fold(jnp.where(eye, f, 0.0)), axis=0, keepdims=True))
            for part in range(2):
                at = (2 * side + jnp.where(core == 0, part, 1 - part)) * half + start
                at = pl.ds(pl.multiple_of(at, STEP), STEP)
                sums[at, j * tile : (j + 1) * tile] = jnp.concatenate(traces[part], axis=0)
        return tuple(energies)

    zero = jnp.zeros((SUB, tile), jnp.float32)
    steps = half // STEP
    energies = lax.fori_loop(0, steps, chunk, (zero,) * count, unroll=steps if count <= 4 else 1)
    spare = pl.ds(pl.multiple_of((1 - side) * 2 * half, SUB), SUB)
    for j in range(count):
        sums[spare, j * tile : (j + 1) * tile] = energies[j]


def walker_rows(sums, occ):
    rows, lanes = sums.shape
    walkers = lanes // occ
    block = lax.broadcasted_iota(jnp.int32, (walkers, lanes), 1) // occ
    owner = lax.broadcasted_iota(jnp.int32, (walkers, lanes), 0)
    ones = (block == owner).astype(jnp.bfloat16)
    parts = []
    for _ in range(3):
        parts.append(sums.astype(jnp.bfloat16))
        sums = sums - parts[-1].astype(jnp.float32)
    total = rows_dot(ones, jnp.concatenate(parts, axis=0))
    return total[:, :rows] + total[:, rows : 2 * rows] + total[:, 2 * rows :]


def own_kernel(greens, partner, own):
    own[0] = greens[0]
    own[1] = partner[0]


def walker_ids(tiles):
    me = lax.axis_index("walk")
    chip, core = me // 2, me % 2
    plain = core == chip % 2
    ids = []
    for tile in tiles:
        if isinstance(tile, tuple):
            ids += [me ^ SINGLES[name] for name in tile]
        else:
            there = chip ^ jnp.where(plain, tile, tile - 1)
            lead = jnp.where(plain, core, 1 - core)
            ids += [2 * there + lead, 2 * there + 1 - lead]
    return ids


def values_of(tiles, refs):
    refs = list(refs)
    values = []
    for tile in tiles:
        if isinstance(tile, tuple):
            values.append(jnp.stack([refs.pop(0)[0] for _ in tile]))
        else:
            values.append(refs.pop(0)[...])
    return values


def send(sent, rows, ids):
    devices = sent.shape[0]
    for r, walker in enumerate(ids):
        for near in range(NEAR):
            to = lax.rem(walker + 1 - near + devices, devices)
            sent[to, :, near * LANES : (near + 1) * LANES] = rows[r : r + 1]


def compute_kernel(tiles, *refs):
    blocks, (mine, other, before, sent, sums) = refs[:-5], refs[-5:]
    me = lax.axis_index("walk")
    block_sums(values_of(tiles, blocks), mine, other, sums, (me // 2) % 2, me % 2)
    sent[...] = before[...]
    send(sent, walker_rows(sums[...], blocks[0].shape[1]), walker_ids(tiles))


def copy_kernel(x, y):
    y[...] = x[...]


def blank_kernel(sent):
    sent[...] = jnp.zeros_like(sent)


def picks(source, counts, slots):
    me = lax.axis_index("walk")
    devices = counts.shape[1]
    count = jnp.sum(jnp.where(lax.broadcasted_iota(jnp.int32, counts.shape, 1) == me, counts[...], 0), axis=1, keepdims=True)
    row = lax.broadcasted_iota(jnp.int32, (NEAR, LANES), 0)
    found = []
    for t in range(slots):
        walker = jnp.where(lax.broadcasted_iota(jnp.int32, source.shape, 1) == t, source[...], 0)
        near = jnp.sum(walker, axis=1, keepdims=True) - me + 1
        near = jnp.where(near < 0, near + devices, jnp.where(near >= devices, near - devices, near))
        found.append(jnp.where((row == near) & (count > t), 1.0, 0.0))
    return found


def relocate(shifts, pick, own, cross, blocks, relocated):
    me = lax.axis_index("walk")
    chip, core = me // 2, me % 2
    chips = lax.axis_size("walk") // 2
    shift = chip ^ lax.rem(chip + jnp.where(core == 0, chips - 1, 1), chips)
    outer = cross[0]
    for s, block in zip(shifts, blocks):
        outer = jnp.where(shift == s, block[1], outer)
    before, after = jnp.where(core == 0, outer, own[1]), jnp.where(core == 0, own[1], outer)
    for t in range(relocated.shape[0]):
        value = jnp.zeros(relocated.shape[1:], jnp.float32)
        for near, walker in enumerate((before, own[0], after)):
            weight = jnp.concatenate([pick[t][near : near + 1]] * (relocated.shape[2] // LANES), axis=1)
            value = jnp.where(weight > 0, walker.astype(jnp.float32), value)
        relocated[t] = value.astype(relocated.dtype)


def final_kernel(scale, shifts, source, counts, got, own, cross, *refs):
    pick = picks(source, counts, refs[-1].shape[0])
    blocks, (relocated, energy, bias) = refs[:-3], refs[-3:]
    relocate(shifts, pick, own, cross, blocks, relocated)
    devices = got.shape[0]
    low = lax.broadcasted_iota(jnp.int32, pick[0].shape, 1) < LANES // 2
    parts = jnp.zeros(pick[0].shape, jnp.float32)
    for q in range(devices // 4):
        even = got[4 * q] + got[4 * q + 1]
        odd = got[4 * q + 2] + got[4 * q + 3]
        even, odd = (jnp.concatenate([x[:, r * LANES : (r + 1) * LANES] for r in range(NEAR)], axis=0) for x in (even, odd))
        tile = jnp.where(low, even, odd)
        parts += jnp.where(low, odd, even)
        for t in range(bias.shape[0]):
            bias[t : t + 1, q * LANES : (q + 1) * LANES] = jnp.sum(tile * pick[t], axis=0, keepdims=True)
    for t in range(bias.shape[0]):
        energy[t] = jnp.sum(parts * pick[t]) * scale


def body(greens, source, counts, cholesky):
    devices = lax.axis_size("walk")
    chips = devices // 2
    chol_dev, occ, orb = cholesky.shape
    slots = source.shape[0]
    nchol = chol_dev * devices
    assert greens.shape[0] == 1 and 4 * chol_dev == LANES and 2 * occ == LANES
    assert chips >= 8 and chips & (chips - 1) == 0
    vmem = pl.BlockSpec(memory_space=pltpu.VMEM)
    smem = pl.BlockSpec(memory_space=pltpu.SMEM)
    params = pltpu.CompilerParams(vmem_limit_bytes=20 * 2**20)

    def permuted(x, source_of):
        return lax.ppermute(x, "walk", [(2 * n + k, 2 * m + c) for m in range(chips) for c in range(2) for n, k in [source_of(m, c)]])

    def trade(s):
        return permuted(own, lambda m, c: (m ^ s, c) if c == m % 2 else (m ^ (s - 1), 1 - c))

    partner = permuted(greens, lambda m, c: (m, 1 - c))
    payload = jax.ShapeDtypeStruct((devices, 1, NEAR * LANES), jnp.float32)
    half = permuted(greens, lambda m, c: (m ^ 4, c))
    blank = pl.pallas_call(
        blank_kernel,
        out_shape=payload,
        out_specs=vmem,
        compiler_params=params,
        cost_estimate=pl.CostEstimate(flops=4 * 10**9, bytes_accessed=4096, transcendentals=0),
    )()
    partner, blank = lax.optimization_barrier((partner, blank))
    own = pl.pallas_call(
        own_kernel,
        out_shape=jax.ShapeDtypeStruct((2, occ, orb), greens.dtype),
        in_specs=[vmem, vmem],
        out_specs=vmem,
        compiler_params=params,
        cost_estimate=pl.CostEstimate(flops=0, bytes_accessed=4 * occ * orb, transcendentals=0),
    )(greens, partner)
    after_own, own = lax.optimization_barrier((cholesky, own))
    other = permuted(after_own, lambda m, c: (m, 1 - c))
    far = trade(7)
    near = trade(3)
    more = list(range(9, chips, 2))
    held = {7: far, 3: near, **{s: trade(s) for s in more}}
    forwarded = permuted(half, lambda m, c: (m ^ 1, c))
    cross = permuted(greens, lambda m, c: (m ^ 1, 1 - c))
    shifts = [2**k - 1 for k in range(2, chips.bit_length())]
    blank = pl.pallas_call(
        copy_kernel,
        out_shape=payload,
        in_specs=[vmem],
        out_specs=vmem,
        compiler_params=params,
        cost_estimate=pl.CostEstimate(flops=4 * 10**9, bytes_accessed=4096, transcendentals=0),
    )(blank)
    singles = {"own": own, "cross": cross, "half": half, "forwarded": forwarded}

    def compute(tiles, before):
        flops = 2 * (2 * len(tiles) * occ) * (2 * chol_dev * occ) * orb
        operands = []
        for tile in tiles:
            operands += [singles[name] for name in tile] if isinstance(tile, tuple) else [held[tile]]
        operands += [cholesky, other, before]
        return pl.pallas_call(
            functools.partial(compute_kernel, tiles),
            out_shape=payload,
            in_specs=[vmem] * len(operands),
            out_specs=vmem,
            scratch_shapes=[pltpu.VMEM((LANES, 2 * len(tiles) * occ), jnp.float32)],
            compiler_params=params,
            cost_estimate=pl.CostEstimate(flops=flops, bytes_accessed=4 * chol_dev * occ * orb, transcendentals=0),
        )(*operands)

    sent = compute([("own", "half"), 3] + more, blank)
    sent = compute([7, ("cross", "forwarded")], sent)
    got = lax.all_to_all(sent, "walk", split_axis=0, concat_axis=0, tiled=True)
    relocated, energy, force_bias = pl.pallas_call(
        functools.partial(final_kernel, -(0.5 / nchol), shifts),
        out_shape=(
            jax.ShapeDtypeStruct((slots, occ, orb), greens.dtype),
            jax.ShapeDtypeStruct((slots,), jnp.float32),
            jax.ShapeDtypeStruct((slots, nchol), jnp.float32),
        ),
        in_specs=[vmem] * (5 + len(shifts)),
        out_specs=[vmem, smem, vmem],
        compiler_params=params,
    )(source.reshape(1, -1), counts.reshape(1, -1), got, own, cross, *[held[s] for s in shifts])
    return relocated, energy, force_bias


def solution(mesh):
    return jax.shard_map(
        body,
        mesh=mesh,
        in_specs=(
            P(("rep", "walk"), None, None),
            P(("rep", "walk")),
            P("rep"),
            P("walk", None, None),
        ),
        out_specs=(P(("rep", "walk"), None, None), P(("rep", "walk")), P(("rep", "walk"), None)),
        check_vma=False,
    )
```

```python
import functools

import jax
import jax.numpy as jnp
from jax import lax
from jax.experimental import pallas as pl
from jax.experimental.pallas import tpu as pltpu
from jax.sharding import PartitionSpec as P

ROWS = (((1,), (1,)), ((), ()))
LANES = 128
SUB = 8
NEAR = 3
SINGLES = {"own": 0, "cross": 3, "half": 8, "forwarded": 10}
STEP = 8


def rows_dot(a, b):
    return lax.dot_general(a, b, ROWS, preferred_element_type=jnp.float32)


def fold(x):
    return jnp.sum(x.reshape(x.shape[0] // SUB, SUB, x.shape[1]), axis=0)


def block_sums(blocks, ca, cb, sums, side, core):
    _, occ, orb = blocks[0].shape
    half = ca.shape[0]
    tile = 2 * occ
    lane = lax.broadcasted_iota(jnp.int32, (occ, tile), 1)
    row = lax.broadcasted_iota(jnp.int32, (occ, tile), 0)
    low = lane < occ
    eye = (lane == row) | (lane - occ == row)
    count = len(blocks)
    walkers = [jnp.concatenate(blocks[j : j + 2], axis=0).reshape(-1, orb) for j in range(0, count, 2)]
    spare = pl.ds(pl.multiple_of((1 - side) * 2 * half, 2 * half), 2 * half)
    sums[spare, :] = jnp.zeros((2 * half, count * tile), jnp.float32)

    def chunk(k, energies):
        energies = list(energies)
        start = pl.multiple_of(k * STEP, STEP)
        va = ca[pl.ds(start, STEP)].reshape(STEP * occ, orb)
        vb = cb[pl.ds(start, STEP)].reshape(STEP * occ, orb)
        for j in range(count):
            if j % 2 == 0:
                fa = rows_dot(va, walkers[j // 2])
                fb = rows_dot(vb, walkers[j // 2])
            cols = slice((j % 2) * tile, (j % 2 + 1) * tile)
            traces = [[], []]
            for i in range(STEP):
                rows = slice(i * occ, (i + 1) * occ)
                f0, f1 = fa[rows, cols], fb[rows, cols]
                turned = jnp.transpose(jnp.concatenate([f0, f1], axis=0))
                t0, t1 = turned[:occ], turned[occ:]
                crossed = pltpu.roll(jnp.where(low, t1, t0), occ, 1)
                energies[j] += fold(f0 * jnp.where(low, t0, crossed) + f1 * jnp.where(low, crossed, t1))
                for part, f in enumerate((f0, f1)):
                    traces[part].append(jnp.sum(fold(jnp.where(eye, f, 0.0)), axis=0, keepdims=True))
            for part in range(2):
                at = (2 * side + jnp.where(core == 0, part, 1 - part)) * half + start
                at = pl.ds(pl.multiple_of(at, STEP), STEP)
                sums[at, j * tile : (j + 1) * tile] = jnp.concatenate(traces[part], axis=0)
        return tuple(energies)

    zero = jnp.zeros((SUB, tile), jnp.float32)
    steps = half // STEP
    energies = lax.fori_loop(0, steps, chunk, (zero,) * count, unroll=steps if count <= 4 else 1)
    spare = pl.ds(pl.multiple_of((1 - side) * 2 * half, SUB), SUB)
    for j in range(count):
        sums[spare, j * tile : (j + 1) * tile] = energies[j]


def walker_rows(sums, occ):
    rows, lanes = sums.shape
    walkers = lanes // occ
    block = lax.broadcasted_iota(jnp.int32, (walkers, lanes), 1) // occ
    owner = lax.broadcasted_iota(jnp.int32, (walkers, lanes), 0)
    ones = (block == owner).astype(jnp.bfloat16)
    parts = []
    for _ in range(3):
        parts.append(sums.astype(jnp.bfloat16))
        sums = sums - parts[-1].astype(jnp.float32)
    total = rows_dot(ones, jnp.concatenate(parts, axis=0))
    return total[:, :rows] + total[:, rows : 2 * rows] + total[:, 2 * rows :]


def own_kernel(greens, partner, own):
    own[0] = greens[0]
    own[1] = partner[0]


def walker_ids(tiles):
    me = lax.axis_index("walk")
    chip, core = me // 2, me % 2
    plain = core == chip % 2
    ids = []
    for tile in tiles:
        if isinstance(tile, tuple):
            ids += [me ^ SINGLES[name] for name in tile]
        else:
            there = chip ^ jnp.where(plain, tile, tile - 1)
            lead = jnp.where(plain, core, 1 - core)
            ids += [2 * there + lead, 2 * there + 1 - lead]
    return ids


def values_of(tiles, refs):
    refs = list(refs)
    values = []
    for tile in tiles:
        if isinstance(tile, tuple):
            values.append(jnp.stack([refs.pop(0)[0] for _ in tile]))
        else:
            values.append(refs.pop(0)[...])
    return values


def send(sent, rows, ids):
    devices = sent.shape[0]
    for r, walker in enumerate(ids):
        for near in range(NEAR):
            sent[lax.rem(walker + 1 - near + devices, devices), near : near + 1, :] = rows[r : r + 1]


def compute_kernel(tiles, *refs):
    blocks, (mine, other, before, sent, sums) = refs[:-5], refs[-5:]
    me = lax.axis_index("walk")
    block_sums(values_of(tiles, blocks), mine, other, sums, (me // 2) % 2, me % 2)
    sent[...] = before[...]
    send(sent, walker_rows(sums[...], blocks[0].shape[1]), walker_ids(tiles))


def copy_kernel(x, y):
    y[...] = x[...]


def blank_kernel(sent):
    sent[...] = jnp.zeros_like(sent)


def picks(source, counts, slots):
    me = lax.axis_index("walk")
    devices = counts.shape[1]
    count = jnp.sum(jnp.where(lax.broadcasted_iota(jnp.int32, counts.shape, 1) == me, counts[...], 0), axis=1, keepdims=True)
    row = lax.broadcasted_iota(jnp.int32, (NEAR, LANES), 0)
    found = []
    for t in range(slots):
        walker = jnp.where(lax.broadcasted_iota(jnp.int32, source.shape, 1) == t, source[...], 0)
        near = jnp.sum(walker, axis=1, keepdims=True) - me + 1
        near = jnp.where(near < 0, near + devices, jnp.where(near >= devices, near - devices, near))
        found.append(jnp.where((row == near) & (count > t), 1.0, 0.0))
    return found


def relocate(shifts, pick, own, cross, blocks, relocated):
    me = lax.axis_index("walk")
    chip, core = me // 2, me % 2
    chips = lax.axis_size("walk") // 2
    shift = chip ^ lax.rem(chip + jnp.where(core == 0, chips - 1, 1), chips)
    outer = cross[0]
    for s, block in zip(shifts, blocks):
        outer = jnp.where(shift == s, block[1], outer)
    before, after = jnp.where(core == 0, outer, own[1]), jnp.where(core == 0, own[1], outer)
    for t in range(relocated.shape[0]):
        value = jnp.zeros(relocated.shape[1:], jnp.float32)
        for near, walker in enumerate((before, own[0], after)):
            weight = jnp.concatenate([pick[t][near : near + 1]] * (relocated.shape[2] // LANES), axis=1)
            value = jnp.where(weight > 0, walker.astype(jnp.float32), value)
        relocated[t] = value.astype(relocated.dtype)


def relocate_kernel(shifts, pick, own, cross, *refs):
    relocate(shifts, pick, own, cross, refs[:-1], refs[-1])


def final_kernel(scale, shifts, source, counts, got, own, cross, *refs):
    pick = picks(source, counts, refs[-1].shape[0])
    blocks, (relocated, energy, bias) = refs[:-3], refs[-3:]
    relocate(shifts, pick, own, cross, blocks, relocated)
    devices = got.shape[0]
    low = lax.broadcasted_iota(jnp.int32, pick[0].shape, 1) < LANES // 2
    parts = jnp.zeros(pick[0].shape, jnp.float32)
    for q in range(devices // 4):
        even = got[4 * q] + got[4 * q + 1]
        odd = got[4 * q + 2] + got[4 * q + 3]
        tile = jnp.where(low, even, odd)
        parts += jnp.where(low, odd, even)
        for t in range(bias.shape[0]):
            bias[t : t + 1, q * LANES : (q + 1) * LANES] = jnp.sum(tile * pick[t], axis=0, keepdims=True)
    for t in range(bias.shape[0]):
        energy[t] = jnp.sum(parts * pick[t]) * scale


def body(greens, source, counts, cholesky):
    devices = lax.axis_size("walk")
    chips = devices // 2
    chol_dev, occ, orb = cholesky.shape
    slots = source.shape[0]
    nchol = chol_dev * devices
    assert greens.shape[0] == 1 and 4 * chol_dev == LANES and 2 * occ == LANES
    assert chips >= 8 and chips & (chips - 1) == 0
    vmem = pl.BlockSpec(memory_space=pltpu.VMEM)
    smem = pl.BlockSpec(memory_space=pltpu.SMEM)
    params = pltpu.CompilerParams(vmem_limit_bytes=20 * 2**20)

    def permuted(x, source_of):
        return lax.ppermute(x, "walk", [(2 * n + k, 2 * m + c) for m in range(chips) for c in range(2) for n, k in [source_of(m, c)]])

    def trade(s):
        return permuted(own, lambda m, c: (m ^ s, c) if c == m % 2 else (m ^ (s - 1), 1 - c))

    partner = permuted(greens, lambda m, c: (m, 1 - c))
    payload = jax.ShapeDtypeStruct((devices, NEAR, LANES), jnp.float32)
    half = permuted(greens, lambda m, c: (m ^ 4, c))
    blank = pl.pallas_call(
        blank_kernel,
        out_shape=payload,
        out_specs=vmem,
        compiler_params=params,
        cost_estimate=pl.CostEstimate(flops=4 * 10**9, bytes_accessed=4096, transcendentals=0),
    )()
    partner, blank = lax.optimization_barrier((partner, blank))
    own = pl.pallas_call(
        own_kernel,
        out_shape=jax.ShapeDtypeStruct((2, occ, orb), greens.dtype),
        in_specs=[vmem, vmem],
        out_specs=vmem,
        compiler_params=params,
        cost_estimate=pl.CostEstimate(flops=0, bytes_accessed=4 * occ * orb, transcendentals=0),
    )(greens, partner)
    other = permuted(cholesky, lambda m, c: (m, 1 - c))
    far = trade(7)
    near = trade(3)
    more = list(range(9, chips, 2))
    held = {7: far, 3: near, **{s: trade(s) for s in more}}
    forwarded = permuted(half, lambda m, c: (m ^ 1, c))
    cross = permuted(greens, lambda m, c: (m ^ 1, 1 - c))
    shifts = [2**k - 1 for k in range(2, chips.bit_length())]
    blank = pl.pallas_call(
        copy_kernel,
        out_shape=payload,
        in_specs=[vmem],
        out_specs=vmem,
        compiler_params=params,
        cost_estimate=pl.CostEstimate(flops=4 * 10**9, bytes_accessed=4096, transcendentals=0),
    )(blank)
    singles = {"own": own, "cross": cross, "half": half, "forwarded": forwarded}

    def compute(tiles, before):
        flops = 2 * (2 * len(tiles) * occ) * (2 * chol_dev * occ) * orb
        operands = []
        for tile in tiles:
            operands += [singles[name] for name in tile] if isinstance(tile, tuple) else [held[tile]]
        operands += [cholesky, other, before]
        return pl.pallas_call(
            functools.partial(compute_kernel, tiles),
            out_shape=payload,
            in_specs=[vmem] * len(operands),
            out_specs=vmem,
            scratch_shapes=[pltpu.VMEM((LANES, 2 * len(tiles) * occ), jnp.float32)],
            compiler_params=params,
            cost_estimate=pl.CostEstimate(flops=flops, bytes_accessed=4 * chol_dev * occ * orb, transcendentals=0),
        )(*operands)

    sent = compute([("own","half"),3] + more, blank)
    sent = compute([7,("cross","forwarded")], sent)
    got = lax.all_to_all(sent, "walk", split_axis=0, concat_axis=0, tiled=True)
    relocated, energy, force_bias = pl.pallas_call(
        functools.partial(final_kernel, -(0.5 / nchol), shifts),
        out_shape=(
            jax.ShapeDtypeStruct((slots, occ, orb), greens.dtype),
            jax.ShapeDtypeStruct((slots,), jnp.float32),
            jax.ShapeDtypeStruct((slots, nchol), jnp.float32),
        ),
        in_specs=[vmem] * (5 + len(shifts)),
        out_specs=[vmem, smem, vmem],
        compiler_params=params,
    )(source.reshape(1, -1), counts.reshape(1, -1), got, own, cross, *[held[s] for s in shifts])
    return relocated, energy, force_bias


def solution(mesh):
    return jax.shard_map(
        body,
        mesh=mesh,
        in_specs=(
            P(("rep", "walk"), None, None),
            P(("rep", "walk")),
            P("rep"),
            P("walk", None, None),
        ),
        out_specs=(P(("rep", "walk"), None, None), P(("rep", "walk")), P(("rep", "walk"), None)),
        check_vma=False,
    )
```
